32 devices in a mesh: section: 2 (over x), expert: 16 (over z, y, core).
Axes of the slice: x: 2, y: 2, z: 4, core: 2. Of those that a mesh axis runs over, the one named last changes fastest.
Arguments:
- queries: bfloat16 [2, 512, 36864], P('section', None, 'expert'), may hold values from -48 to 48
- stretch_latents: bfloat16 [2, 512, 576], P('section', 'expert'), may hold values from -6 to 6
- pool_latents: bfloat16 [2, 3072, 576], P('section', 'expert'), may hold values from -6 to 6
- stretch_offset: int32 [2], P('section'), may hold values from 0 to 3072
- value_up: bfloat16 [2, 64, 512, 128], P('section', 'expert'), may hold values from -0.75 to 0.75
- out_proj: bfloat16 [2, 8192, 7168], P('section', 'expert'), may hold values from -0.25 to 0.25
- resid: bfloat16 [2, 512, 7168], P('section', 'expert'), may hold values from -6 to 6
- norm_gain: float32 [2, 7168], P('section'), may hold values from 0.1 to 1.9
- expert_ids: int32 [2, 512, 2], P('section', 'expert'), may hold values from 0 to 1, all different within a row; in each aligned block of 32 rows (0 to 31, 32 to 63, ..., all dimensions but the last counted through in order) at most 32 rows name the same one
- route_weight: float32 [2, 512, 2], P('section', 'expert'), may hold values from 0.05 to 1
- gate_up: bfloat16 [2, 16, 7168, 2, 128], P('section', 'expert'), may hold values from -0.0625 to 0.0625
- down_proj: bfloat16 [2, 16, 128, 7168], P('section', 'expert'), may hold values from -0.1875 to 0.1875
- page_owner: int32 [2, 32], P('section', 'expert'), may hold values from 0 to 1
Outputs:
- layer_out: bfloat16 [2, 512, 7168], P('section', 'expert')
- page_store: bfloat16 [2, 32, 2, 9216], P('section', 'expert')
The draws below stay inside these ranges and needn't reach their ends.
Inputs may be any that keep to these rules, and one draw needn't show every extreme that they name: `expert_ids`: in the 32 tokens of one device no expert is named by more than 32 tokens.
All inputs are finite; a program needn't handle non-finite values.
Results may differ from the reference program's by a relative error of at most 0.029.
Values may be sent and summed in bfloat16 or wider, within the bound.
No kernel may reach another device: no remote copies, remote signals or barrier semaphores. Data moves between devices by JAX's collectives and lax.ppermute only.
A program may use at most 128 MiB of HBM per device.

```python
import math
import jax
import jax.numpy as jnp
import numpy as np
from jax import lax

D = 7168
HEADS = 64
LAT = 512
ROPE = 64
LATW = 576
HEAD_DIM = 128
FF_E = 1024
EXP_SPAN = 8
HID_DEV = 128
EXPERTS = 2
TOPK = 2
STRETCH = 512
POOL = 3072
PAGE = 16
T_DEV = 32
CAP = 32
N_SECTION = 2
N_EXPERT = 16


def shared_latents(key):
    base = jnp.clip(jax.random.normal(jax.random.fold_in(key, 101), (N_SECTION, STRETCH, LATW), jnp.float32), -6.0, 6.0)
    return base


def draw_stretch_latents(key, part):
    base = shared_latents(key)
    return base.astype(jnp.bfloat16)


def draw_queries(key, part):
    key = jax.random.fold_in(key, 5)
    values = jnp.clip(jax.random.normal(key, (N_SECTION, STRETCH, HEADS * LATW), jnp.float32), -6.0, 6.0)
    return values.astype(jnp.bfloat16)


def touch_ends(values, own_key, least, high):
    longest = values.shape.index(max(values.shape))
    spots = []
    for shift in (0, 1):
        where = [jax.random.randint(jax.random.fold_in(own_key, axis), (), 0, length) for axis, length in enumerate(values.shape)]
        where[longest] = (where[longest] + shift) % values.shape[longest]
        spots.append(tuple(where))
    return values.at[spots[0]].set(least).at[spots[1]].set(high)


def shard_levels(key, dims, shards, low, high):
    def one(axis_at, shards_of):
        draws = jax.random.uniform(jax.random.fold_in(jax.random.fold_in(key, 6), axis_at), (shards_of,), jnp.float32, low / len(shards), high / len(shards))
        return jnp.repeat(jnp.exp(draws), dims[axis_at] // shards_of).reshape((-1,) + (1,) * (len(dims) - axis_at - 1))

    loudness = one(*shards[0])
    for cut in shards[1:]:
        loudness = loudness * one(*cut)
    return loudness


def assign_block(rng, own, number, rows, number_of, top, reach, slope):
    order = jax.random.permutation(rng, number_of)
    crowded, common = load_shares(number_of, rows * top, reach, slope, True), load_shares(number_of, rows * top, reach, slope, False)
    places = jnp.arange(number_of)

    def named(sizes, turn):
        used = int((sizes > 0).sum())
        fixed = max(1, used // 4)
        shifted = fixed + (places - fixed + turn * (used - fixed)) % max(1, number_of - fixed)
        return jnp.zeros((number_of,), jnp.int32).at[order[jnp.where(places < fixed, places, shifted)]].set(jnp.asarray(sizes, jnp.int32))

    sizes = jnp.where(number % 4 == 0, named(crowded, number // 4), named(common, number - number // 4 - 1))
    mixed = jax.random.permutation(jax.random.fold_in(own, 3), number_of)
    source_of, receiver = mixed[0:number_of // 2 * 2:2], mixed[1:number_of // 2 * 2:2]
    room = jnp.minimum(sizes[source_of] - 1, reach - sizes[receiver]) // 2
    room = jnp.where((source_of == order[0]) | (receiver == order[0]) | (sizes[receiver] == 0), 0, jnp.maximum(room, 0))
    shifted = jax.random.randint(jax.random.fold_in(own, 4), (number_of // 2,), 0, 1 << 20) % (room + 1)
    sizes = sizes.at[source_of].add(-shifted).at[receiver].add(shifted)
    items = jnp.searchsorted(jnp.cumsum(sizes), jnp.arange(rows * top), side="right").astype(jnp.int32)
    table = items.reshape(top, rows).T
    table = table[jax.random.permutation(jax.random.fold_in(own, 1), rows)]
    turn = jax.random.randint(jax.random.fold_in(own, 2), (rows, 1), 0, top)
    return jnp.take_along_axis(table, (jnp.arange(top)[None, :] + turn) % top, axis=1)


def load_shares(amount, total, bound, lean, full):
    loads = [(1 << 20) // math.isqrt(rank ** lean) + 1 for rank in range(1, amount + 1)]
    largest = bound if full else min(bound, max(-(-total // amount), total * loads[0] // sum(loads)))
    least = 1 if total - largest >= amount - 1 else 0
    holding, spare = [largest] + [least] * (amount - 1), total - largest - least * (amount - 1)
    while spare > 0:
        free = [i for i in range(1, amount) if holding[i] < largest] or [i for i in range(1, amount) if holding[i] < bound]
        mass, remaining = sum([loads[i] for i in free]), spare
        for i in free:
            extra = min(bound - holding[i], max(1, remaining * loads[i] // mass), spare)
            holding[i] = holding[i] + extra
            spare = spare - extra
    return np.array(holding)


def bell_draw(key, extent, scale, reach, shards=(), held_as=jnp.bfloat16):
    gain = shard_levels(key, extent, shards, -0.22, 0.18) if shards else 1.0
    drawn = jax.random.normal(key, extent, jnp.float32) * scale * gain
    return jnp.minimum(jnp.maximum(drawn, -reach), reach).astype(held_as)


def setup_inputs(seed: int = 0) -> dict:
    arg_keys = jax.random.split(jax.random.key(seed), 14)
    queries = draw_queries(jax.random.fold_in(arg_keys[13], 71), 0)
    stretch_latents = draw_stretch_latents(jax.random.fold_in(arg_keys[13], 71), 0)
    pool_latents = bell_draw(arg_keys[2], (N_SECTION, POOL, LATW), 1.0, 6.0, ((0, 2), (1, 16)))
    stretch_offset = jax.random.randint(arg_keys[3], (N_SECTION,), 0, POOL + 1).astype(jnp.int32)
    value_up = bell_draw(arg_keys[4], (N_SECTION, HEADS, LAT, HEAD_DIM), (LAT // 8) ** -0.5, 0.75, ((0, 2), (1, 16)))
    out_proj = bell_draw(arg_keys[5], (N_SECTION, HEADS * HEAD_DIM, D), (HEADS * HEAD_DIM // 16) ** -0.5, 0.25, ((0, 2), (1, 16)))
    resid = bell_draw(arg_keys[6], (N_SECTION, STRETCH, D), 1.0, 6.0, ((0, 2), (1, 16)))
    norm_gain = jnp.clip(1.0 + 0.18 * jax.random.normal(arg_keys[7], (N_SECTION, D), jnp.float32), 0.1, 1.9)
    expert_ids_keys = jax.random.split(jax.random.fold_in(arg_keys[8], 1), N_SECTION * STRETCH // T_DEV)
    expert_ids_turns = jax.random.permutation(jax.random.fold_in(arg_keys[8], 3), N_SECTION * STRETCH // T_DEV)
    expert_ids = jax.vmap(lambda own, number: assign_block(jax.random.fold_in(arg_keys[8], 2), own, number, T_DEV, EXPERTS, TOPK, CAP, 2))(expert_ids_keys, expert_ids_turns).reshape((N_SECTION, STRETCH, TOPK))
    route_weight = jnp.clip(jnp.exp(math.log(1.0) - 2.9957323 * jax.random.uniform(arg_keys[9], (N_SECTION, STRETCH, TOPK), jnp.float32) ** shard_levels(arg_keys[9], (N_SECTION, STRETCH, TOPK), ((0, 2), (1, 16)), -0.2, 0.2)), 0.05, 1.0)
    gate_up = bell_draw(arg_keys[10], (N_SECTION, N_EXPERT, D, 2, HID_DEV), D ** -0.5, 0.0625, ((0, 2), (1, 16)))
    down_proj = bell_draw(arg_keys[11], (N_SECTION, N_EXPERT, HID_DEV, D), FF_E ** -0.5, 0.1875, ((0, 2), (1, 16)))
    page_owner = touch_ends(jax.random.randint(arg_keys[12], (N_SECTION, STRETCH // PAGE), 0, N_SECTION), jax.random.fold_in(arg_keys[12], 1), 0, N_SECTION - 1).astype(jnp.int32)
    return dict(queries=queries, stretch_latents=stretch_latents, pool_latents=pool_latents, stretch_offset=stretch_offset, value_up=value_up, out_proj=out_proj, resid=resid, norm_gain=norm_gain, expert_ids=expert_ids, route_weight=route_weight, gate_up=gate_up, down_proj=down_proj, page_owner=page_owner)


def attend(query, keys, offset):
    position = jnp.arange(POOL + STRETCH, dtype=jnp.int32)
    token = jnp.arange(STRETCH, dtype=jnp.int32)
    visible = jnp.where((position < POOL)[None, :], (position < offset)[None, :], (position - POOL)[None, :] <= token[:, None])
    scores = jnp.dot(query, keys.T, preferred_element_type=jnp.float32) * (1.0 / math.sqrt(HEAD_DIM + ROPE))
    top = lax.optimization_barrier(jnp.max(jnp.where(visible, scores, -1e+30), axis=1, keepdims=True))
    probs = jnp.where(visible, jnp.exp(scores - top), 0.0)
    denom = lax.optimization_barrier(jnp.sum(probs, axis=1, keepdims=True))
    mixed = jnp.dot(probs.astype(jnp.bfloat16), keys[:, :LAT], preferred_element_type=jnp.float32) / denom
    return mixed.astype(jnp.bfloat16)

def reference(queries, stretch_latents, pool_latents, stretch_offset, value_up, out_proj, resid, norm_gain, expert_ids, route_weight, gate_up, down_proj, page_owner):
    groups = HEADS // N_EXPERT
    outputs = []
    pages_all = []
    for section_idx in range(N_SECTION):
        keys = jnp.concatenate([pool_latents[section_idx], stretch_latents[section_idx]], axis=0)
        query = queries[section_idx].reshape(STRETCH, HEADS, LATW)
        offset = stretch_offset[section_idx]

        def head(h):
            latent = attend(query[:, h, :], keys, offset)
            return jnp.dot(latent, value_up[section_idx, h], preferred_element_type=jnp.float32).astype(jnp.bfloat16)
        heads_out = lax.map(head, jnp.arange(HEADS, dtype=jnp.int32))
        grouped = heads_out.reshape(N_EXPERT, groups, STRETCH, HEAD_DIM)
        weights_out = out_proj[section_idx].reshape(N_EXPERT, groups * HEAD_DIM, D)

        def add_group(total, pair):
            block, weight = pair
            rows = block.transpose(1, 0, 2).reshape(STRETCH, groups * HEAD_DIM)
            term = jnp.dot(rows, weight, preferred_element_type=jnp.float32).astype(jnp.bfloat16).astype(jnp.float32)
            return (total + term, None)
        attn, _ = lax.scan(add_group, jnp.zeros((STRETCH, D), jnp.float32), (grouped, weights_out))
        mid = resid[section_idx].astype(jnp.float32) + attn
        normed = (mid * lax.rsqrt(lax.optimization_barrier(jnp.mean(mid * mid, axis=-1, keepdims=True)) + 1e-06) * norm_gain[section_idx]).astype(jnp.bfloat16)
        scores_r = route_weight[section_idx]
        share = (2.827 * scores_r / lax.optimization_barrier(jnp.sum(scores_r, axis=-1, keepdims=True))).astype(jnp.bfloat16)
        chosen = (expert_ids[section_idx][:, :, None] == jnp.arange(EXPERTS, dtype=jnp.int32)).astype(jnp.float32)
        table = lax.optimization_barrier(jnp.sum(chosen * share.astype(jnp.float32)[:, :, None], axis=1))

        def add_slice(total, j):
            expert = j // EXP_SPAN
            weight_in = gate_up[section_idx, j].reshape(D, 2 * HID_DEV)
            both = jnp.dot(normed, weight_in, preferred_element_type=jnp.float32)
            gate = both[:, :HID_DEV]
            upper = both[:, HID_DEV:]
            factor = lax.optimization_barrier(jnp.sum(table * (jnp.arange(EXPERTS, dtype=jnp.int32) == expert), axis=1))
            hidden = (factor[:, None] * (jax.nn.silu(gate) * upper)).astype(jnp.bfloat16)
            part = jnp.dot(hidden, down_proj[section_idx, j], preferred_element_type=jnp.float32).astype(jnp.bfloat16).astype(jnp.float32)
            return (total + part, None)
        moe, _ = lax.scan(add_slice, jnp.zeros((STRETCH, D), jnp.float32), jnp.arange(N_EXPERT, dtype=jnp.int32))
        outputs.append((mid + moe).astype(jnp.bfloat16))
        pages_all.append(stretch_latents[section_idx].reshape(STRETCH // PAGE, PAGE * LATW))
    layer_out = jnp.stack(outputs, axis=0)
    pages = jnp.stack(pages_all, axis=0).transpose(1, 0, 2)
    owners = page_owner.T
    match = owners[None, :, :] == jnp.arange(N_SECTION, dtype=jnp.int32)[:, None, None]
    page_store = jnp.where(match[:, :, :, None], pages[None], jnp.zeros((), jnp.bfloat16)).astype(jnp.bfloat16)
    return (layer_out, page_store)
```

```python
import functools
import math

import jax
import jax.numpy as jnp
from jax import lax
from jax.experimental import pallas as pl
from jax.experimental.pallas import tpu as pltpu
from jax.sharding import PartitionSpec as P

LAT = 512
ROPE = 64
LATW = 576
WIDE = 640
HEAD_DIM = 128
EXP_SPAN = 8
PAGE = 16
NEVER = -1e30
FLOOR = -1e29
VMEM = 26 * 1024 * 1024


def chip_at(place, chips):
    return jnp.where(place < chips // 2, 2 * place, 2 * (chips - 1 - place) + 1)


def place_of(chip, chips):
    return jnp.where(chip % 2 == 0, chip // 2, chips - 1 - chip // 2)


def offsets_of(chips):
    listed = [chips // 2]
    for far in range(chips // 2 - 1, 0, -1):
        listed += [far, -far]
    return listed + [0]


def key_groups(chips):
    arrive = [0] + [x for far in range(1, chips // 2) for x in (far, -far)] + [chips // 2]
    cut = 1 + 2 * (chips // 4)
    return arrive[:cut], arrive[cut:]


def shard_at(me, offset, other, chips):
    core = lax.rem(me, 2)
    if other:
        core = 1 - core
    place = place_of(lax.div(me, 2), chips)
    return chip_at(lax.rem(place + offset + chips, chips), chips) * 2 + core


def zero_of(x):
    return jnp.minimum(jnp.abs(x.astype(jnp.float32)), 0.0)


def pack_kernel(stretch, pool, ids, weight, first, second):
    tok = stretch.shape[0]
    cut = first.shape[1]
    first[:tok, :] = stretch[:, :cut]
    first[tok:, :] = pool[:, :cut]
    second[:, LAT - cut :] = jnp.zeros((second.shape[0], WIDE - LAT), second.dtype)
    second[:tok, : LATW - cut] = stretch[:, cut:]
    second[tok:, : LATW - cut] = pool[:, cut:]
    scores = weight[...]
    share = 2.827 * scores / jnp.sum(scores, axis=0, keepdims=True)
    share = share.astype(jnp.bfloat16).astype(jnp.float32)
    lane = lax.broadcasted_iota(jnp.int32, (tok, WIDE - LATW), 1)
    turn = lax.broadcasted_iota(jnp.int32, (tok, tok), 0) == lax.broadcasted_iota(
        jnp.int32, (tok, tok), 1
    )
    table = jnp.zeros((tok, WIDE - LATW), jnp.float32)
    for k in range(ids.shape[0]):
        chosen = jnp.sum(jnp.where(turn, ids[k : k + 1, :], 0), axis=1, keepdims=True)
        part = jnp.sum(jnp.where(turn, share[k : k + 1, :], 0.0), axis=1, keepdims=True)
        table = table + jnp.where(lane == chosen, part, 0.0)
    second[:tok, LATW - cut :] = table.astype(second.dtype)


def join_kernel(*refs):
    pieces, out = refs[:-1], refs[-1]
    rows, cut = pieces[0].shape
    for i in range(len(pieces) // 2):
        out[i * rows : (i + 1) * rows, :cut] = pieces[2 * i][...]
        out[i * rows : (i + 1) * rows, cut:] = pieces[2 * i + 1][...]


def attend_kernel(chips, tok, pool_here, heads, part, meta, queries, value_up, *refs):
    half = chips // 2
    offsets = offsets_of(chips)
    held = [offset for group in key_groups(chips) for offset in group]
    joined = refs[:4]
    out = refs[4]
    at = 5
    if part == 0:
        factor = refs[at]
        at += 1
    qs, pool, near, acc, peak, denom = refs[at:]
    me, offset = meta[0], meta[1]
    span = half * pool_here
    many = chips * tok
    whole = lax.div(offset, pool_here)
    early = len(key_groups(chips)[0])

    def piece(kind, s, rows):
        block = joined[kind * 2 + (0 if s < early else 1)]
        at_row = (s if s < early else s - early) * (tok + pool_here)
        return block[at_row + rows.start : at_row + rows.stop, :]

    count = jnp.int32(0)
    blank = jnp.int32(0)
    for kind in range(2):
        for s in range(chips):
            shard = shard_at(me, held[s], kind == 1, chips)
            at_row = (kind * chips + s) * tok
            near[at_row : at_row + tok, :] = piece(kind, s, slice(0, tok))
            shown = shard * pool_here < offset
            slot = jnp.where(shard == whole, whole, count)

            @pl.when(shown)
            def _(kind=kind, s=s, slot=slot):
                start = pl.multiple_of(slot * pool_here, 16)
                pool[pl.ds(start, pool_here), :] = piece(kind, s, slice(tok, tok + pool_here))

            @pl.when(jnp.logical_not(shown))
            def _(blank=blank):
                start = pl.multiple_of((2 * chips - 1 - blank) * pool_here, 16)
                pool[pl.ds(start, pool_here), :] = jnp.zeros((pool_here, WIDE), pool.dtype)

            count = count + (shard < whole).astype(jnp.int32)
            blank = blank + 1 - shown.astype(jnp.int32)
    if part == 0:
        for s in range(chips):
            at_row = offsets.index(held[s]) * tok
            factor[at_row : at_row + tok, :] = piece(0, s, slice(0, tok))[:, LAT:]

    qs[:, LAT:] = jnp.zeros((heads * many, WIDE - LAT), qs.dtype)
    for i in range(chips):
        shard = shard_at(me, offsets[part * half + i % half], i < half, chips)
        rows = pl.ds(pl.multiple_of(shard * tok, 16), tok)
        for h in range(heads):
            to = h * many + i * tok
            qs[to : to + tok, :LATW] = queries[rows, h * LATW : (h + 1) * LATW]
    acc[...] = jnp.zeros_like(acc)
    peak[...] = jnp.full(peak.shape, FLOOR, jnp.float32)
    denom[...] = jnp.zeros_like(denom)
    factor2 = math.log2(math.e) / math.sqrt(HEAD_DIM + ROPE)
    chains = [slice(h * many, (h + 1) * many) for h in range(heads)]

    def absorb(keys, hide):
        scores = [
            lax.dot_general(
                qs[cut, :], keys, (((1,), (1,)), ((), ())), preferred_element_type=jnp.float32
            )
            for cut in chains
        ]
        for cut, s in zip(chains, scores):
            s = hide(s)
            old = peak[cut, :1]
            new = jnp.maximum(old, jnp.max(s, axis=1, keepdims=True))
            probs = jnp.exp2((s - new) * factor2)
            fade = jnp.exp2((old - new) * factor2)
            denom[cut, :] = denom[cut, :] * fade + jnp.sum(probs, axis=1, keepdims=True)
            acc[cut, :] = acc[cut, :] * fade + jnp.dot(
                probs.astype(jnp.bfloat16), keys[:, :LAT], preferred_element_type=jnp.float32
            )
            peak[cut, :] = jnp.broadcast_to(new, (many, peak.shape[1]))

    row = lax.broadcasted_iota(jnp.int32, (many, 1), 0)
    col = lax.broadcasted_iota(jnp.int32, (1, 2 * chips * tok), 1)
    row_tok = row
    for i in range(chips):
        shard = shard_at(me, offsets[part * half + i % half], i < half, chips)
        row_tok = jnp.where(row // tok == i, row + (shard - i) * tok, row_tok)
    col_tok = col
    for i in range(2 * chips):
        shard = shard_at(me, held[i % chips], i >= chips, chips)
        col_tok = jnp.where(col // tok == i, col + (shard - i) * tok, col_tok)
    absorb(near[...], lambda s: jnp.where(col_tok <= row_tok, s, NEVER))

    def pool_keys(block):
        return pool[pl.ds(pl.multiple_of(block * span, 16), span), :]

    def pool_block(block, carry):
        absorb(pool_keys(block), lambda s: s)
        return carry

    blocks = lax.div(offset, span)
    left = offset - blocks * span
    lax.fori_loop(0, blocks, pool_block, 0)

    @pl.when(left > 0)
    def _():
        lane = lax.broadcasted_iota(jnp.int32, (1, span), 1)
        absorb(pool_keys(blocks), lambda s: jnp.where(lane < left, s, NEVER))

    for h, cut in enumerate(chains):
        latent = (acc[cut, :] / denom[cut, :1]).astype(jnp.bfloat16)
        out[:, h * HEAD_DIM : (h + 1) * HEAD_DIM] = jnp.dot(
            latent, value_up[h], preferred_element_type=jnp.float32
        ).astype(out.dtype)


def attend(meta, queries, joined, value_up, part, chips):
    heads = value_up.shape[0]
    tok = queries.shape[0] // (2 * chips)
    pool_here = (joined[0].shape[0] + joined[1].shape[0]) // chips - tok
    many = chips * tok
    out_shape = [jax.ShapeDtypeStruct((many, heads * HEAD_DIM), jnp.bfloat16)]
    if part == 0:
        out_shape.append(jax.ShapeDtypeStruct((many, WIDE - LAT), jnp.bfloat16))
    keys = 2 * chips * (tok + pool_here)
    vmem = pl.BlockSpec(memory_space=pltpu.VMEM)
    return pl.pallas_call(
        functools.partial(attend_kernel, chips, tok, pool_here, heads, part),
        in_specs=[pl.BlockSpec(memory_space=pltpu.SMEM)] + [vmem] * (2 + len(joined)),
        out_specs=[vmem] * len(out_shape),
        scratch_shapes=[
            pltpu.VMEM((heads * many, WIDE), jnp.bfloat16),
            pltpu.VMEM((2 * chips * pool_here, WIDE), jnp.bfloat16),
            pltpu.VMEM((2 * chips * tok, WIDE), jnp.bfloat16),
            pltpu.VMEM((heads * many, LAT), jnp.float32),
            pltpu.VMEM((heads * many, 128), jnp.float32),
            pltpu.VMEM((heads * many, 128), jnp.float32),
        ],
        out_shape=out_shape,
        compiler_params=pltpu.CompilerParams(vmem_limit_bytes=VMEM),
        cost_estimate=pl.CostEstimate(
            flops=2 * heads * many * keys * (WIDE + LAT),
            bytes_accessed=keys * WIDE * 2 + queries.size * 2,
            transcendentals=heads * many * keys,
        ),
    )(meta, queries, value_up, *joined)


def body(
    queries,
    stretch_latents,
    pool_latents,
    stretch_offset,
    value_up,
    out_proj,
    resid,
    norm_gain,
    expert_ids,
    route_weight,
    gate_up,
    down_proj,
    page_owner,
):
    width_all = lax.axis_size("expert")
    sections = lax.axis_size("section")
    tok_here = stretch_latents.shape[1]
    row_dev = pool_latents.shape[1] + tok_here
    experts_n = width_all // EXP_SPAN
    me = lax.axis_index("expert")
    chips = width_all // 2
    half = chips // 2
    many = half * tok_here
    order = list(range(0, chips, 2)) + list(range(chips - 1, 0, -2))
    upwards = [
        (order[p] * 2 + c, order[(p + 1) % chips] * 2 + c) for p in range(chips) for c in range(2)
    ]
    downwards = [(b, a) for a, b in upwards]
    offsets = offsets_of(chips)
    siblings = [(d, d ^ 1) for d in range(width_all)]

    def swap(x):
        return lax.ppermute(x, "expert", siblings)

    def reach(lane):
        return (half - lane % 2, half - 1 + lane % 2)

    def ring_gather(lanes):
        got = {0: list(lanes)}
        up, down = list(lanes), list(lanes)
        for step in range(1, half + 1):
            for lane in range(len(lanes)):
                if step <= reach(lane)[0]:
                    up[lane] = lax.ppermute(up[lane], "expert", upwards)
                    got.setdefault(half if step == half else -step, []).append(up[lane])
                if step <= reach(lane)[1]:
                    down[lane] = lax.ppermute(down[lane], "expert", downwards)
                    got.setdefault(step, []).append(down[lane])
        return got

    def lane_cuts(lanes):
        cols = resid.shape[2] // lanes
        return [slice(lane * cols, (lane + 1) * cols) for lane in range(lanes)]

    def ring_reduce(terms):
        pieces = []
        for lane, term in enumerate(terms):
            total = term[0].astype(jnp.float32)
            for pairs, sign, hops in zip((upwards, downwards), (1, -1), reach(lane)):
                part = term[half if hops == half else sign * hops]
                for far in range(hops, 0, -1):
                    moved = lax.ppermute(part, "expert", pairs).astype(jnp.float32)
                    if far > 1:
                        part = moved + term[sign * (far - 1)].astype(jnp.float32)
                        part = part.astype(jnp.bfloat16)
                total = total + moved
            pieces.append(total)
        return jnp.concatenate(pieces, axis=1)

    def dot(x, y):
        return jnp.dot(x, y, preferred_element_type=jnp.float32)

    front = 384
    packed = pl.pallas_call(
        pack_kernel,
        out_shape=[
            jax.ShapeDtypeStruct((row_dev, front), jnp.bfloat16),
            jax.ShapeDtypeStruct((row_dev, WIDE - front), jnp.bfloat16),
        ],
    )(stretch_latents[0], pool_latents[0], expert_ids[0].T, route_weight[0].T)
    got = ring_gather(packed)
    joined = []
    for group in key_groups(chips):
        pieces = [x for offset in group for x in got[offset]]
        joined.append(
            pl.pallas_call(
                join_kernel,
                out_shape=jax.ShapeDtypeStruct((len(group) * row_dev, WIDE), jnp.bfloat16),
            )(*pieces)
        )
    joined += [swap(x) for x in joined]
    out_pair = [out_proj[0], swap(out_proj[0])]
    down_pair = [down_proj[0, 0], swap(down_proj[0, 0])]
    ready = zero_of(out_pair[1][0, 0]).astype(jnp.int32)
    meta = jnp.stack([me, stretch_offset[0] + ready]).astype(jnp.int32)
    hid_here = gate_up.shape[4]
    lanes = lane_cuts(2)
    terms = [{} for _ in lanes]

    def project(heads):
        own, sibling = heads[many:], swap(heads[:many])
        return [
            (dot(own, out_pair[0][:, cut]) + dot(sibling, out_pair[1][:, cut])).astype(jnp.bfloat16)
            for cut in lanes
        ]

    def extend(blocks, part):
        for lane, block in zip(terms, blocks):
            for i, offset in enumerate(offsets[part * half : (part + 1) * half]):
                lane[offset] = block[i * tok_here : (i + 1) * tok_here]

    head_first, table = attend(meta, queries[0], joined, value_up[0], 0, chips)
    blocks, meta = lax.optimization_barrier((project(head_first), meta))
    extend(blocks, 0)
    head_late = attend(meta, queries[0], joined, value_up[0], 1, chips)[0]
    extend(project(head_late), 1)
    flat = gate_up[0, 0].reshape(gate_up.shape[2], 2 * hid_here)
    flat = flat + zero_of(head_late[0, 0]).astype(jnp.bfloat16)
    flat_pair = [flat, swap(flat)]
    weight_down = jnp.concatenate(down_pair, axis=0)
    attn = ring_reduce(terms)
    mid = resid[0].astype(jnp.float32) + attn
    normed = (
        mid * lax.rsqrt(jnp.mean(mid * mid, axis=-1, keepdims=True) + 1e-06) * norm_gain[0]
    ).astype(jnp.bfloat16)
    pick = (jnp.arange(experts_n, dtype=jnp.int32) == me // EXP_SPAN).astype(jnp.float32)
    factors = jnp.sum(
        table[:, LATW - LAT : LATW - LAT + experts_n].astype(jnp.float32) * pick, axis=1
    )
    got = ring_gather([normed[:, cut] for cut in lanes])
    terms = [{} for _ in lanes]
    for i, offset in enumerate(offsets):
        factor = factors[i * tok_here : (i + 1) * tok_here, None]
        if i in (1, 2):
            factor = factor + sum(zero_of(x[0, 0]) for x in got[half])
        hidden = []
        for flat in flat_pair:
            both = sum(dot(x, flat[cut]) for x, cut in zip(got[offset], lanes))
            hidden.append(factor * (jax.nn.silu(both[:, :hid_here]) * both[:, hid_here:]))
        hidden = jnp.concatenate(hidden, axis=1).astype(jnp.bfloat16)
        for lane, cut in zip(terms, lanes):
            lane[offset] = dot(hidden, weight_down[:, cut]).astype(jnp.bfloat16)
    moe = ring_reduce(terms)
    layer_out = (mid + moe).astype(jnp.bfloat16)[None]
    pages_here = tok_here // PAGE
    owner_late = page_owner + zero_of(attn[0, 0]).astype(jnp.int32)
    latent_pages = stretch_latents[0].reshape(pages_here, PAGE * LATW)
    owner_hot = owner_late[0][:, None] == jnp.arange(sections, dtype=jnp.int32)
    outgoing = jnp.where(
        owner_hot[:, :, None], latent_pages[:, None, :], jnp.zeros((), jnp.bfloat16)
    )
    if sections == 2:
        first = lax.axis_index("section") == 0
        stay = jnp.where(first, outgoing[:, 0], outgoing[:, 1])
        leave = jnp.where(first, outgoing[:, 1], outgoing[:, 0])
        come = lax.ppermute(leave, "section", [(0, 1), (1, 0)])
        page_store = jnp.stack(
            [jnp.where(first, stay, come), jnp.where(first, come, stay)], axis=1
        )[None]
    else:
        page_store = lax.all_to_all(outgoing, "section", split_axis=1, concat_axis=1, tiled=True)[
            None
        ]
    return (layer_out, page_store)


def solution(mesh):
    placed = (
        P("section", None, "expert"),
        P("section", "expert", None),
        P("section", "expert", None),
        P("section"),
        P("section", "expert", None, None),
        P("section", "expert", None),
        P("section", "expert", None),
        P("section", None),
        P("section", "expert", None),
        P("section", "expert", None),
        P("section", "expert", None, None, None),
        P("section", "expert", None, None),
        P("section", "expert"),
    )
    return jax.shard_map(
        body,
        mesh=mesh,
        in_specs=placed,
        out_specs=(P("section", "expert", None), P("section", "expert", None, None)),
        check_vma=False,
    )
```

```python
import functools
import math

import jax
import jax.numpy as jnp
from jax import lax
from jax.experimental import pallas as pl
from jax.experimental.pallas import tpu as pltpu
from jax.sharding import PartitionSpec as P

LAT = 512
ROPE = 64
LATW = 576
WIDE = 640
HEAD_DIM = 128
EXP_SPAN = 8
PAGE = 16
NEVER = -1e30
FLOOR = -1e29
VMEM = 46 * 1024 * 1024
TILE = 1792


def chip_at(place, chips):
    return jnp.where(place < chips // 2, 2 * place, 2 * (chips - 1 - place) + 1)


def place_of(chip, chips):
    return jnp.where(chip % 2 == 0, chip // 2, chips - 1 - chip // 2)


def offsets_of(chips):
    listed = [chips // 2]
    for far in range(chips // 2 - 1, 0, -1):
        listed += [far, -far]
    return listed + [0]


def shard_at(me, offset, other, chips):
    core = lax.rem(me, 2)
    if other:
        core = 1 - core
    place = place_of(lax.div(me, 2), chips)
    return chip_at(lax.rem(place + offset + chips, chips), chips) * 2 + core


def zero_of(x):
    return jnp.minimum(jnp.abs(x.astype(jnp.float32)), 0.0)


def pack_kernel(stretch, pool, ids, weight, first, second):
    tok = stretch.shape[0]
    cut = first.shape[1]
    first[:tok, :] = stretch[:, :cut]
    first[tok:, :] = pool[:, :cut]
    second[:, LAT - cut :] = jnp.zeros((second.shape[0], WIDE - LAT), second.dtype)
    second[:tok, : LATW - cut] = stretch[:, cut:]
    second[tok:, : LATW - cut] = pool[:, cut:]
    scores = weight[...]
    share = 2.827 * scores / jnp.sum(scores, axis=0, keepdims=True)
    share = share.astype(jnp.bfloat16).astype(jnp.float32)
    lane = lax.broadcasted_iota(jnp.int32, (tok, WIDE - LATW), 1)
    turn = lax.broadcasted_iota(jnp.int32, (tok, tok), 0) == lax.broadcasted_iota(
        jnp.int32, (tok, tok), 1
    )
    table = jnp.zeros((tok, WIDE - LATW), jnp.float32)
    for k in range(ids.shape[0]):
        chosen = jnp.sum(jnp.where(turn, ids[k : k + 1, :], 0), axis=1, keepdims=True)
        part = jnp.sum(jnp.where(turn, share[k : k + 1, :], 0.0), axis=1, keepdims=True)
        table = table + jnp.where(lane == chosen, part, 0.0)
    second[:tok, LATW - cut :] = table.astype(second.dtype)


def join_kernel(*refs):
    pieces, out = refs[:-1], refs[-1]
    rows, cut = pieces[0].shape
    for i in range(len(pieces) // 2):
        out[i * rows : (i + 1) * rows, :cut] = pieces[2 * i][...]
        out[i * rows : (i + 1) * rows, cut:] = pieces[2 * i + 1][...]


def join(pieces):
    rows = len(pieces) // 2 * pieces[0].shape[0]
    return pl.pallas_call(
        join_kernel, out_shape=jax.ShapeDtypeStruct((rows, WIDE), jnp.bfloat16)
    )(*pieces)


def queries_kernel(chips, tok, heads, meta, queries, *outs):
    many = chips * tok
    for kind, out in enumerate(outs):
        out[:, LAT:] = jnp.zeros((out.shape[0], WIDE - LAT), out.dtype)
        for i, offset in enumerate(offsets_of(chips)):
            shard = shard_at(meta[0], offset, kind == 1, chips)
            rows = pl.ds(pl.multiple_of(shard * tok, 16), tok)
            for h in range(heads):
                to = h * many + i * tok
                out[to : to + tok, :LATW] = queries[rows, h * LATW : (h + 1) * LATW]


def attend_kernel(chips, tok, pool_here, heads, lanes, meta, *refs):
    half = chips // 2
    offsets = offsets_of(chips)
    queries, value_up = refs[0:2], refs[2:4]
    joined, weights = refs[4:6], refs[6:8]
    outs = refs[8 : 8 + lanes * chips]
    factor, pool, near, acc, peak, denom, head, held, near_sem, pool_sem, held_sem = refs[
        8 + lanes * chips :
    ]
    me, offset = meta[0], meta[1]
    span = half * pool_here
    many = chips * tok
    rows_dev = tok + pool_here
    whole = lax.div(offset, pool_here)

    near_copies, pool_copies, held_copies = [], [], []
    count = jnp.int32(0)
    blank = jnp.int32(0)
    for kind in range(2):
        for s in range(chips):
            i = kind * chips + s
            shard = shard_at(me, offsets[s], kind == 1, chips)
            shown = shard * pool_here < offset
            slot = jnp.where(shard == whole, whole, count)
            slot = jnp.where(shown, slot, 2 * chips - 1 - blank)
            start = pl.multiple_of(slot * pool_here, 16)
            block, top = joined[kind], s * rows_dev
            near_copies.append(
                pltpu.make_async_copy(
                    block.at[top : top + tok, :], near.at[i * tok : (i + 1) * tok, :], near_sem.at[i]
                )
            )
            pool_copies.append(
                pltpu.make_async_copy(
                    block.at[top + tok : top + rows_dev, :],
                    pool.at[pl.ds(start, pool_here), :],
                    pool_sem.at[i],
                )
            )
            count = count + (shard < whole).astype(jnp.int32)
            blank = blank + 1 - shown.astype(jnp.int32)
    depth = weights[0].shape[0]
    chunk = depth // 4
    for kind in range(2):
        for i in range(4):
            rows = slice(i * chunk, (i + 1) * chunk)
            held_copies.append(
                pltpu.make_async_copy(
                    weights[kind].at[rows, :],
                    held.at[kind * depth + rows.start : kind * depth + rows.stop, :],
                    held_sem.at[kind * 4 + i],
                )
            )
    for copy in near_copies + pool_copies + held_copies:
        copy.start()
    acc[...] = jnp.zeros_like(acc)
    peak[...] = jnp.full(peak.shape, FLOOR, jnp.float32)
    denom[...] = jnp.zeros_like(denom)
    factor2 = math.log2(math.e) / math.sqrt(HEAD_DIM + ROPE)
    chains = [slice(h * many, (h + 1) * many) for h in range(2 * heads)]
    groups = [range(0, heads), range(heads, 2 * heads)]

    def absorb(group, keys, hide):
        scores = [
            lax.dot_general(
                queries[h // heads][chains[h % heads], :],
                keys,
                (((1,), (1,)), ((), ())),
                preferred_element_type=jnp.float32,
            )
            for h in group
        ]
        for h, s in zip(group, scores):
            cut = chains[h]
            s = hide(s)
            old = peak[cut, :1]
            new = jnp.maximum(old, jnp.max(s, axis=1, keepdims=True))
            probs = jnp.exp2((s - new) * factor2)
            fade = jnp.exp2((old - new) * factor2)
            denom[cut, :] = denom[cut, :] * fade + jnp.sum(probs, axis=1, keepdims=True)
            acc[cut, :] = acc[cut, :] * fade + jnp.dot(
                probs.astype(jnp.bfloat16), keys[:, :LAT], preferred_element_type=jnp.float32
            )
            peak[cut, :] = jnp.broadcast_to(new, (many, peak.shape[1]))

    for copy in near_copies:
        copy.wait()
    for s in range(chips):
        factor[s * tok : (s + 1) * tok, :] = near[s * tok : (s + 1) * tok, LAT:]

    row = lax.broadcasted_iota(jnp.int32, (many, 1), 0)
    col = lax.broadcasted_iota(jnp.int32, (1, 2 * many), 1)
    row_tok, col_tok = row, col
    for i in range(2 * chips):
        shard = shard_at(me, offsets[i % chips], i >= chips, chips)
        col_tok = jnp.where(col // tok == i, col + (shard - i) * tok, col_tok)
        if i < chips:
            row_tok = jnp.where(row // tok == i, row + (shard - i) * tok, row_tok)
    for group in groups:
        absorb(group, near[...], lambda s: jnp.where(col_tok <= row_tok, s, NEVER))

    for copy in pool_copies:
        copy.wait()

    def pool_keys(block):
        return pool[pl.ds(pl.multiple_of(block * span, 16), span), :]

    def pool_block(block, carry):
        for group in groups:
            absorb(group, pool_keys(block), lambda s: s)
        return carry

    blocks = lax.div(offset, span)
    left = offset - blocks * span
    lax.fori_loop(0, blocks, pool_block, 0)

    @pl.when(left > 0)
    def _():
        lane = lax.broadcasted_iota(jnp.int32, (1, span), 1)
        for group in groups:
            absorb(group, pool_keys(blocks), lambda s: jnp.where(lane < left, s, NEVER))

    for h, cut in enumerate(chains):
        latent = (acc[cut, :] / denom[cut, :1]).astype(jnp.bfloat16)
        head[:, h * HEAD_DIM : (h + 1) * HEAD_DIM] = jnp.dot(
            latent, value_up[h // heads][h % heads], preferred_element_type=jnp.float32
        ).astype(head.dtype)

    for copy in held_copies:
        copy.wait()
    cols = outs[0].shape[1]
    for lane in range(lanes):
        for left in range(0, cols, TILE):
            block = jnp.dot(
                head[...],
                held[:, lane * cols + left : lane * cols + left + TILE],
                preferred_element_type=jnp.float32,
            )
            for i in range(chips):
                outs[lane * chips + i][:, left : left + TILE] = block[
                    i * tok : (i + 1) * tok
                ].astype(outs[0].dtype)


def order_queries(meta, queries, heads, chips):
    vmem = pl.BlockSpec(memory_space=pltpu.VMEM)
    tok = queries.shape[0] // (2 * chips)
    return pl.pallas_call(
        functools.partial(queries_kernel, chips, tok, heads),
        in_specs=[pl.BlockSpec(memory_space=pltpu.SMEM), vmem],
        out_specs=[vmem] * 2,
        out_shape=[jax.ShapeDtypeStruct((heads * chips * tok, WIDE), jnp.bfloat16)] * 2,
    )(meta, queries)


def attend(meta, queries, value_up, joined, weights, tok, chips, lanes):
    heads = value_up[0].shape[0]
    pool_here = joined[0].shape[0] // chips - tok
    many = chips * tok
    vmem = pl.BlockSpec(memory_space=pltpu.VMEM)
    keys = 2 * chips * (tok + pool_here)
    depth, wide = weights[0].shape
    return pl.pallas_call(
        functools.partial(attend_kernel, chips, tok, pool_here, heads, lanes),
        in_specs=[pl.BlockSpec(memory_space=pltpu.SMEM)]
        + [vmem] * 4
        + [pl.BlockSpec(memory_space=pl.ANY)] * 4,
        out_specs=[vmem] * (lanes * chips + 1),
        scratch_shapes=[
            pltpu.VMEM((2 * chips * pool_here, WIDE), jnp.bfloat16),
            pltpu.VMEM((2 * many, WIDE), jnp.bfloat16),
            pltpu.VMEM((2 * heads * many, LAT), jnp.float32),
            pltpu.VMEM((2 * heads * many, 128), jnp.float32),
            pltpu.VMEM((2 * heads * many, 128), jnp.float32),
            pltpu.VMEM((many, 2 * depth), jnp.bfloat16),
            pltpu.VMEM((2 * depth, wide), jnp.bfloat16),
            pltpu.SemaphoreType.DMA((2 * chips,)),
            pltpu.SemaphoreType.DMA((2 * chips,)),
            pltpu.SemaphoreType.DMA((8,)),
        ],
        out_shape=[jax.ShapeDtypeStruct((tok, wide // lanes), jnp.bfloat16)] * (lanes * chips)
        + [jax.ShapeDtypeStruct((many, WIDE - LAT), jnp.bfloat16)],
        compiler_params=pltpu.CompilerParams(vmem_limit_bytes=VMEM),
        cost_estimate=pl.CostEstimate(
            flops=4 * heads * many * keys * (WIDE + LAT) + 4 * many * depth * wide,
            bytes_accessed=keys * WIDE * 2 + 4 * depth * wide,
            transcendentals=2 * heads * many * keys,
        ),
    )(meta, *queries, *value_up, *joined, *weights)


def body(
    queries,
    stretch_latents,
    pool_latents,
    stretch_offset,
    value_up,
    out_proj,
    resid,
    norm_gain,
    expert_ids,
    route_weight,
    gate_up,
    down_proj,
    page_owner,
):
    width_all = lax.axis_size("expert")
    sections = lax.axis_size("section")
    tok_here = stretch_latents.shape[1]
    row_dev = pool_latents.shape[1] + tok_here
    experts_n = width_all // EXP_SPAN
    me = lax.axis_index("expert")
    chips = width_all // 2
    half = chips // 2
    many = half * tok_here
    order = list(range(0, chips, 2)) + list(range(chips - 1, 0, -2))
    upwards = [
        (order[p] * 2 + c, order[(p + 1) % chips] * 2 + c) for p in range(chips) for c in range(2)
    ]
    downwards = [(b, a) for a, b in upwards]
    offsets = offsets_of(chips)
    siblings = [(d, d ^ 1) for d in range(width_all)]

    def swap(x):
        return lax.ppermute(x, "expert", siblings)

    def reach(lane):
        return (half - lane % 2, half - 1 + lane % 2)

    def ring_gather(lanes):
        got = {0: list(lanes)}
        up, down = list(lanes), list(lanes)
        for step in range(1, half + 1):
            for lane in range(len(lanes)):
                if step <= reach(lane)[0]:
                    up[lane] = lax.ppermute(up[lane], "expert", upwards)
                    got.setdefault(half if step == half else -step, []).append(up[lane])
                if step <= reach(lane)[1]:
                    down[lane] = lax.ppermute(down[lane], "expert", downwards)
                    got.setdefault(step, []).append(down[lane])
        return got

    def lane_cuts(lanes):
        cols = resid.shape[2] // lanes
        return [slice(lane * cols, (lane + 1) * cols) for lane in range(lanes)]

    def ring_reduce(terms):
        pieces, came = [], []
        for lane, term in enumerate(terms):
            total = term[0].astype(jnp.float32)
            for pairs, sign, hops in zip((upwards, downwards), (1, -1), reach(lane)):
                part = term[half if hops == half else sign * hops]
                for far in range(hops, 0, -1):
                    moved = lax.ppermute(part, "expert", pairs).astype(jnp.float32)
                    came.append(moved)
                    if far > 1:
                        part = moved + term[sign * (far - 1)].astype(jnp.float32)
                        part = part.astype(jnp.bfloat16)
                total = total + moved
            pieces.append(total)
        return jnp.concatenate(pieces, axis=1), came

    def dot(x, y):
        return jnp.dot(x, y, preferred_element_type=jnp.float32)

    front = 384
    packed = pl.pallas_call(
        pack_kernel,
        out_shape=[
            jax.ShapeDtypeStruct((row_dev, front), jnp.bfloat16),
            jax.ShapeDtypeStruct((row_dev, WIDE - front), jnp.bfloat16),
        ],
    )(stretch_latents[0], pool_latents[0], expert_ids[0].T, route_weight[0].T)
    got = ring_gather(packed)
    pieces = [x for offset in offsets for x in got[offset]]
    joined = [join(pieces)]
    joined.append(swap(joined[0]))
    out_pair = [out_proj[0], swap(out_proj[0])]
    up_pair = [value_up[0], swap(value_up[0])]
    meta = jnp.stack([me, stretch_offset[0]]).astype(jnp.int32)
    hid_here = gate_up.shape[4]
    lanes = lane_cuts(2)
    gate_pair = (gate_up[0, 0], swap(gate_up[0, 0]))
    flat_pair = [x.reshape(x.shape[0], 2 * hid_here) for x in gate_pair]
    mine, theirs = order_queries(meta, queries[0], value_up.shape[1], chips)
    *blocks, table = attend(
        meta, [mine, swap(theirs)], up_pair, joined, out_pair, tok_here, chips, len(lanes)
    )
    terms = [dict(zip(offsets, blocks[i * chips :])) for i in range(len(lanes))]
    attn, came = ring_reduce(terms)
    later = zero_of(came[1][0, 0])
    down_late = down_proj[0, 0] + later.astype(jnp.bfloat16)
    weight_down = jnp.concatenate([down_proj[0, 0], swap(down_late)], axis=0)
    mid = resid[0].astype(jnp.float32) + attn
    normed = (
        mid * lax.rsqrt(jnp.mean(mid * mid, axis=-1, keepdims=True) + 1e-06) * norm_gain[0]
    ).astype(jnp.bfloat16)
    pick = (jnp.arange(experts_n, dtype=jnp.int32) == me // EXP_SPAN).astype(jnp.float32)
    factors = jnp.sum(
        table[:, LATW - LAT : LATW - LAT + experts_n].astype(jnp.float32) * pick, axis=1
    )
    got = ring_gather([normed[:, cut] for cut in lanes])
    terms = [{} for _ in lanes]
    for i, offset in enumerate(offsets):
        factor = factors[i * tok_here : (i + 1) * tok_here, None]
        if i in (1, 2):
            factor = factor + zero_of(terms[-1][half][0, 0])
        hidden = []
        for flat in flat_pair:
            both = sum(dot(x, flat[cut]) for x, cut in zip(got[offset], lanes))
            hidden.append(factor * (jax.nn.silu(both[:, :hid_here]) * both[:, hid_here:]))
        hidden = jnp.concatenate(hidden, axis=1).astype(jnp.bfloat16)
        for lane, cut in zip(terms, lanes):
            lane[offset] = dot(hidden, weight_down[:, cut]).astype(jnp.bfloat16)
    moe, _ = ring_reduce(terms)
    layer_out = (mid + moe).astype(jnp.bfloat16)[None]
    pages_here = tok_here // PAGE
    owner_late = page_owner + later.astype(jnp.int32)
    latent_pages = stretch_latents[0].reshape(pages_here, PAGE * LATW)
    owner_hot = owner_late[0][:, None] == jnp.arange(sections, dtype=jnp.int32)
    outgoing = jnp.where(
        owner_hot[:, :, None], latent_pages[:, None, :], jnp.zeros((), jnp.bfloat16)
    )
    if sections == 2:
        first = lax.axis_index("section") == 0
        stay = jnp.where(first, outgoing[:, 0], outgoing[:, 1])
        leave = jnp.where(first, outgoing[:, 1], outgoing[:, 0])
        come = lax.ppermute(leave, "section", [(0, 1), (1, 0)])
        page_store = jnp.stack(
            [jnp.where(first, stay, come), jnp.where(first, come, stay)], axis=1
        )[None]
    else:
        page_store = lax.all_to_all(outgoing, "section", split_axis=1, concat_axis=1, tiled=True)[
            None
        ]
    return (layer_out, page_store)


def solution(mesh):
    placed = (
        P("section", None, "expert"),
        P("section", "expert", None),
        P("section", "expert", None),
        P("section"),
        P("section", "expert", None, None),
        P("section", "expert", None),
        P("section", "expert", None),
        P("section", None),
        P("section", "expert", None),
        P("section", "expert", None),
        P("section", "expert", None, None, None),
        P("section", "expert", None, None),
        P("section", "expert"),
    )
    return jax.shard_map(
        body,
        mesh=mesh,
        in_specs=placed,
        out_specs=(P("section", "expert", None), P("section", "expert", None, None)),
        check_vma=False,
    )
```
